32 devices in a mesh: ens: 2 (over y), slab: 16 (over z, x, core).
Axes of the slice: x: 2, y: 2, z: 4, core: 2. Of those that a mesh axis runs over, the one named last changes fastest.
Arguments:
- starting_joint_sensitivities: float32 [8, 2, 128, 65536], P('ens', None, 'slab'), parts along dimension 0, may hold values from -6 to 6
- former_section_velocity: float32 [8, 2, 128, 65536], P('ens', None, 'slab'), parts along dimension 0, may hold values from -6 to 6
- nominal_coefficient_factors: float32 [14], P('ens'), parts along dimension 0, may hold values from 0.5 to 2
- unlocking_coefficients_by_grade: float32 [32], P('ens'), parts along dimension 0, may hold values from 0.2 to 5
- repression_grade_by_abundance: int32 [1024], replicated, may hold values from 0 to 15
- measured_outbreak_frequencies: int32 [128], replicated, may hold values from 1 to 99
- upper_bounds_per_abundance: int32 [128], P('slab'), may hold values from 32 to 64
Outputs:
- section_slope: float32 [8, 2, 128, 65536], P('ens', None, 'slab'), parts along dimension 0
The draws below stay inside these ranges and needn't reach their ends.
There are 2 independent parts, one for each index of `ens`. The reference program is written for one: setup_inputs(seed, part) draws one part's arguments, and reference() takes and returns one part's arrays. A program takes and returns all parts, laid end to end along the dimension named above; an argument that names none is the same for every part. Nothing has to cross between parts.
All inputs are finite; a program needn't handle non-finite values.
Results may differ from the reference program's by a relative error of at most 0.00005.
Values sent between devices are 32-bit elements; how exact they have to be, the bound alone decides.
A program may use at most 576 MiB of HBM per device.

```python
import math
import jax
import jax.numpy as jnp
from jax import lax

TRANSCRIPT_COUNT = 128
COMPONENTS = 4
GENES = 2
KINETIC_VALUES = 7
LEVELS = 16
P1 = 64
P2 = 1024


def plant(result, stream_key, low, top_value):
    dims = result.shape
    index_at = [jax.random.randint(jax.random.fold_in(stream_key, axis), (), 0, dims[axis]) for axis in range(len(dims))]
    result = result.at[tuple(index_at)].set(low)
    longest = dims.index(max(dims))
    index_at[longest] = (index_at[longest] + 1) % dims[longest]
    return result.at[tuple(index_at)].set(top_value)


def block_levels(rng, extent, cuts, least, top_value):
    def one(dim, blocks):
        steps = jax.random.uniform(jax.random.fold_in(jax.random.fold_in(rng, 6), dim), (blocks,), jnp.float32, least / len(cuts), top_value / len(cuts))
        return jnp.repeat(jnp.exp(steps), extent[dim] // blocks).reshape((-1,) + (1,) * (len(extent) - dim - 1))

    loudness = one(*cuts[0])
    for cut in cuts[1:]:
        loudness = loudness * one(*cut)
    return loudness


def bell_draw(rng, shape, scale, limit, split=(), held_as=jnp.bfloat16):
    entries = jax.random.normal(rng, shape, jnp.float32) * scale
    if len(split) > 0:
        entries = block_levels(rng, shape, split, -0.22, 0.18) * entries
    return jnp.clip(entries, min=-limit, max=limit).astype(held_as)


def setup_inputs(seed: int = 0, part: int = 0) -> dict:
    streams_of = jax.random.split(jax.random.key(seed), 8)
    part_keys = jax.random.split(jax.random.fold_in(streams_of[7], part), 8)
    return {
        "starting_joint_sensitivities": bell_draw(part_keys[0], (COMPONENTS, GENES, TRANSCRIPT_COUNT, P1 * P2), 1.0, 6.0, ((2, 16),), jnp.float32),
        "former_section_velocity": bell_draw(part_keys[1], (COMPONENTS, GENES, TRANSCRIPT_COUNT, P1 * P2), 1.0, 6.0, ((2, 16),), jnp.float32),
        "nominal_coefficient_factors": jnp.clip(jnp.exp(jax.random.uniform(part_keys[2], (KINETIC_VALUES,), jnp.float32, math.log(0.5), math.log(2.0))), 0.5, 2.0),
        "unlocking_coefficients_by_grade": jnp.clip(jnp.exp(jax.random.uniform(part_keys[3], (LEVELS,), jnp.float32, math.log(0.2), math.log(5.0))), 0.2, 5.0),
        "repression_grade_by_abundance": plant(jax.random.randint(streams_of[4], (P2,), 0, LEVELS), jax.random.fold_in(streams_of[4], 1), 0, LEVELS - 1).astype(jnp.int32),
        "measured_outbreak_frequencies": plant(jax.random.randint(streams_of[5], (TRANSCRIPT_COUNT,), 1, 100), jax.random.fold_in(streams_of[5], 1), 1, 99).astype(jnp.int32),
        "upper_bounds_per_abundance": plant(jax.random.randint(streams_of[6], (TRANSCRIPT_COUNT,), P1 // 2, P1 + 1), jax.random.fold_in(streams_of[6], 1), P1 // 2, P1).astype(jnp.int32),
    }


nominal_coefficient_basis = (2.0, 0.02, 1.0, 0.01, 0.02, 0.03, 0.002)
section_step = 0.125


def episode_share_stencil(measured_outbreak_frequencies, stencil_breadth):
    episode_extents = jnp.arange(stencil_breadth, dtype=jnp.int32)
    episode_shares = measured_outbreak_frequencies.astype(jnp.float32) * (episode_extents >= 1).astype(jnp.float32)
    episode_shares = episode_shares / jnp.sum(episode_shares)
    backward_difference = episode_extents[:, None] - episode_extents[None, :]
    single_selector = (backward_difference[:, :, None] == episode_extents[None, None, :]).astype(jnp.float32)
    return jnp.dot(single_selector, episode_shares, precision=lax.Precision.HIGHEST)


def kon_rates(unlocking_coefficients_by_grade, repression_grade_by_abundance):
    levels = jnp.arange(unlocking_coefficients_by_grade.shape[0], dtype=jnp.int32)
    single_selector = (repression_grade_by_abundance[:, None] == levels[None, :]).astype(jnp.float32)
    return jnp.dot(single_selector, unlocking_coefficients_by_grade, precision=lax.Precision.HIGHEST)


def shift_lower(field, reduce_axis, amount):
    zero_rim = jnp.zeros_like(lax.slice_in_dim(field, 0, amount, axis=reduce_axis))
    return jnp.concatenate([zero_rim, lax.slice_in_dim(field, 0, field.shape[reduce_axis] - amount, axis=reduce_axis)], axis=reduce_axis)


def shift_upper(field, reduce_axis, amount):
    zero_rim = jnp.zeros_like(lax.slice_in_dim(field, 0, amount, axis=reduce_axis))
    return jnp.concatenate([lax.slice_in_dim(field, amount, field.shape[reduce_axis], axis=reduce_axis), zero_rim], axis=reduce_axis)


def decay_term(field, upper_rows, m_count, coefficient_sequence_values):
    m_grid = m_count[None, None, :, None]
    return coefficient_sequence_values[3] * ((m_grid + 1.0) * upper_rows - m_grid * field)


def section_terms(field, mterm, removal_inflow_term, m_count, coefficient_sequence_values, kon_flat, plane_width):
    episode_jump, peptide_current_term, silencing_constant, transcript_removal, primary_molecule_removal, compose_partner_molecule, partner_molecule_removal = [coefficient_sequence_values[displacement_count] for displacement_count in range(7)]
    cell_total = field.shape[3]
    flat_index = jnp.arange(cell_total, dtype=jnp.int32)
    second_index = flat_index % plane_width
    a_grid = (flat_index // plane_width).astype(jnp.float32)[None, None, None, :]
    c_grid = second_index.astype(jnp.float32)[None, None, None, :]
    below_mask = (second_index >= 1).astype(jnp.float32)[None, None, None, :]
    above_mask = (second_index < plane_width - 1).astype(jnp.float32)[None, None, None, :]
    m_grid = m_count[None, None, :, None]
    opening_constant_array = kon_flat[None, None, None, :]
    lower_a = shift_lower(field, 3, plane_width)
    upper_a = shift_upper(field, 3, plane_width)
    lower_c = shift_lower(field, 3, 1) * below_mask
    upper_c = shift_upper(field, 3, 1) * above_mask
    total = mterm
    total = total + peptide_current_term * m_grid * (lower_a - field)
    total = total + primary_molecule_removal * ((a_grid + 1.0) * upper_a - a_grid * field)
    total = total + compose_partner_molecule * a_grid * (lower_c - field)
    total = total + partner_molecule_removal * ((c_grid + 1.0) * upper_c - c_grid * field)
    silent_block_tensor = field[:, 0:1]
    expressing_block_tensor = field[:, 1:2]
    switch_off = silencing_constant * expressing_block_tensor - opening_constant_array * silent_block_tensor
    opening_current_term = opening_constant_array * silent_block_tensor - silencing_constant * expressing_block_tensor + episode_jump * (removal_inflow_term - expressing_block_tensor)
    total = total + jnp.concatenate([switch_off, opening_current_term], axis=1)
    distribution_tensor = field[0:1]
    expressing_share = distribution_tensor[:, 1:2]
    episode_generator = jnp.concatenate([jnp.zeros_like(expressing_share), episode_jump * (removal_inflow_term[0:1] - expressing_share)], axis=1)
    peptide_generator = peptide_current_term * m_grid * (lower_a[0:1] - distribution_tensor)
    silent_generator = jnp.concatenate([silencing_constant * expressing_share, -silencing_constant * expressing_share], axis=1)
    generator_summands = jnp.concatenate([jnp.zeros_like(distribution_tensor), episode_generator, peptide_generator, silent_generator], axis=0)
    return total + generator_summands


def reference(starting_joint_sensitivities, former_section_velocity, nominal_coefficient_factors, unlocking_coefficients_by_grade, repression_grade_by_abundance, measured_outbreak_frequencies, upper_bounds_per_abundance):
    coefficient_sequence_values = nominal_coefficient_factors * jnp.array(nominal_coefficient_basis, dtype=jnp.float32)
    stencil_breadth = starting_joint_sensitivities.shape[2]
    cell_total = starting_joint_sensitivities.shape[3]
    flat_index = jnp.arange(cell_total, dtype=jnp.int32)
    first_index = flat_index // P2
    second_index = flat_index % P2
    inside = (first_index[None, :] < upper_bounds_per_abundance[:, None]).astype(jnp.float32)
    inside = inside[None, None, :, :]
    solution_tensor = inside * (starting_joint_sensitivities + section_step * former_section_velocity)
    episode_convolution = episode_share_stencil(measured_outbreak_frequencies, stencil_breadth)
    kon = kon_rates(unlocking_coefficients_by_grade, repression_grade_by_abundance)
    plane_levels = jnp.arange(P2, dtype=jnp.int32)
    plane_selector = (second_index[:, None] == plane_levels[None, :]).astype(jnp.float32)
    kon_flat = jnp.dot(plane_selector, kon, precision=lax.Precision.HIGHEST)
    removal_inflow_term = jnp.einsum("vk,loks->lovs", episode_convolution, solution_tensor[:, 1:2], precision=lax.Precision.HIGHEST)
    m_count = jnp.arange(stencil_breadth, dtype=jnp.float32)
    mterm = decay_term(solution_tensor, shift_upper(solution_tensor, 2, 1), m_count, coefficient_sequence_values)
    total = section_terms(solution_tensor, mterm, removal_inflow_term, m_count, coefficient_sequence_values, kon_flat, P2)
    return inside * total
```

```python
import functools

import jax
import jax.numpy as jnp
from jax import lax
from jax.experimental import pallas as pl
from jax.experimental.pallas import tpu as pltpu
from jax.sharding import PartitionSpec as P

P2 = 1024
nominal_coefficient_basis = (2.0, 0.02, 1.0, 0.01, 0.02, 0.03, 0.002)
section_step = 0.125
PLANES = 8
VMEM_LIMIT = 48 * 1024 * 1024
HIGHEST = lax.Precision.HIGHEST


def shifted(value, axis, steps):
    count = lax.axis_size(axis)
    first, last = (max(0, -steps), min(count, count - steps))
    return lax.ppermute(value, axis, [(source, source + steps) for source in range(first, last)])


def episode_share_stencil(measured_outbreak_frequencies, stencil_breadth):
    episode_extents = jnp.arange(stencil_breadth, dtype=jnp.int32)
    episode_shares = measured_outbreak_frequencies.astype(jnp.float32) * (
        episode_extents >= 1
    ).astype(jnp.float32)
    episode_shares = episode_shares / jnp.sum(episode_shares)
    backward_difference = episode_extents[:, None] - episode_extents[None, :]
    single_selector = (backward_difference[:, :, None] == episode_extents[None, None, :]).astype(
        jnp.float32
    )
    return jnp.dot(single_selector, episode_shares, precision=HIGHEST)


def kon_rates(unlocking_coefficients_by_grade, repression_grade_by_abundance):
    levels = jnp.arange(unlocking_coefficients_by_grade.shape[0], dtype=jnp.int32)
    single_selector = (repression_grade_by_abundance[:, None] == levels[None, :]).astype(
        jnp.float32
    )
    return jnp.dot(single_selector, unlocking_coefficients_by_grade, precision=HIGHEST)


def on_state(start, velocity, bound, component, blocks):
    _, _, rows, cells = start.shape
    width = cells // blocks
    per_step = max(1, min(blocks, 8192 // width))
    planes = width // P2 if width >= P2 else 1

    def kernel(bound_ref, start_ref, velocity_ref, out_ref):
        step = pl.program_id(0)
        value = start_ref[...] + section_step * velocity_ref[...]
        cell = step * (per_step * width) + lax.broadcasted_iota(jnp.int32, value.shape, 1)
        value = jnp.where((cell // P2) < bound_ref[:, 0:1], value, 0.0)
        for part in range(per_step):
            out_ref[part] = value[:, part * width : (part + 1) * width]

    spec = pl.BlockSpec((None, None, rows, per_step * width), lambda j: (component, 1, 0, j))
    return pl.pallas_call(
        kernel,
        grid=(blocks // per_step,),
        in_specs=[pl.BlockSpec((rows, 128), lambda j: (0, 0)), spec, spec],
        out_specs=pl.BlockSpec((per_step, rows, width), lambda j: (j, 0, 0)),
        out_shape=jax.ShapeDtypeStruct((blocks, rows, width), jnp.float32),
        compiler_params=pltpu.CompilerParams(vmem_limit_bytes=VMEM_LIMIT),
        cost_estimate=pl.CostEstimate(
            flops=3 * rows * cells, bytes_accessed=12 * rows * cells, transcendentals=0
        ),
    )(bound, start, velocity)


def partial_slope(start, velocity, halo, rates, bound, row_rates, diagonals, columns):
    comps, genes, rows, cells = start.shape
    firsts = cells // P2
    steps = firsts // PLANES

    def kernel(
        rate_ref,
        bound_ref,
        row_ref,
        diagonal_ref,
        column_ref,
        start_ref,
        velocity_ref,
        start_low,
        velocity_low,
        start_high,
        velocity_high,
        halo_ref,
        out_ref,
        state,
    ):
        step = pl.program_id(0)
        off, decay1, make2 = rate_ref[2], rate_ref[4], rate_ref[5]
        first_plane = step * PLANES
        bound_column = bound_ref[:, 0:1]

        def masked(plane, value):
            return jnp.where((bound_column > plane) & (plane >= 0), value, 0.0)

        for comp in range(comps):
            for gene in range(genes):
                state[0, comp, gene] = masked(
                    first_plane - 1,
                    start_low[comp, gene] + section_step * velocity_low[comp, gene],
                )
                high = start_high[comp, gene] + section_step * velocity_high[comp, gene]
                state[PLANES + 1, comp, gene] = jnp.where(
                    first_plane + PLANES < firsts, masked(first_plane + PLANES, high), 0.0
                )

        @pl.loop(0, PLANES)
        def _(plane):
            lanes = pl.ds(pl.multiple_of(plane * P2, P2), P2)
            for comp in range(comps):
                for gene in range(genes):
                    state[plane + 1, comp, gene] = masked(
                        first_plane + plane,
                        start_ref[comp, gene, :, lanes]
                        + section_step * velocity_ref[comp, gene, :, lanes],
                    )

        @pl.loop(0, PLANES)
        def _(plane):
            lanes = pl.ds(pl.multiple_of(plane * P2, P2), P2)
            count = (first_plane + plane).astype(jnp.float32)
            inside = bound_column > first_plane + plane
            trans_m = row_ref[:, 0:1]
            mdecay_up = row_ref[:, 128:129]
            own = -count * (decay1 + make2)
            above_rate = decay1 * (count + 1.0)
            made = (make2 * count) * column_ref[1:2, :]
            removed = column_ref[2:3, :]
            kon = column_ref[0:1, :]
            last_row = lax.broadcasted_iota(jnp.int32, (rows, P2), 0) == rows - 1
            for comp in range(comps):
                silent = state[plane + 1, comp, 0]
                active = state[plane + 1, comp, 1]
                for gene in range(genes):
                    value = silent if gene == 0 else active
                    lower = state[plane, comp, gene]
                    total = (diagonal_ref[gene] + own) * value
                    total = total + trans_m * lower
                    total = total + above_rate * state[plane + 2, comp, gene]
                    total = total + made * pltpu.roll(value, 1, 1)
                    total = total + removed * pltpu.roll(value, P2 - 1, 1)
                    if gene == 0:
                        total = total + off * active
                        beyond = jnp.where(
                            last_row,
                            halo_ref[comp : comp + 1, lanes],
                            pltpu.roll(value, rows - 1, 0),
                        )
                        total = total + mdecay_up * beyond
                    else:
                        total = total + kon * silent
                    if comp == 2:
                        total = total + trans_m * (
                            state[plane, 0, gene] - state[plane + 1, 0, gene]
                        )
                    if comp == 3:
                        source = off * state[plane + 1, 0, 1]
                        total = total + source if gene == 0 else total - source
                    out_ref[comp, gene, :, lanes] = jnp.where(inside, total, 0.0)

    def whole(shape):
        return pl.BlockSpec(shape, lambda i: (0,) * len(shape))

    main = pl.BlockSpec((comps, genes, rows, PLANES * P2), lambda i: (0, 0, 0, i))
    low = pl.BlockSpec((comps, genes, rows, P2), lambda i: (0, 0, 0, jnp.maximum(i * PLANES - 1, 0)))
    high = pl.BlockSpec(
        (comps, genes, rows, P2), lambda i: (0, 0, 0, jnp.minimum((i + 1) * PLANES, firsts - 1))
    )
    return pl.pallas_call(
        kernel,
        grid=(steps,),
        in_specs=[
            pl.BlockSpec(memory_space=pltpu.SMEM),
            whole((rows, 128)),
            whole((rows, 256)),
            whole((genes, rows, P2)),
            whole((8, P2)),
            main,
            main,
            low,
            low,
            high,
            high,
            pl.BlockSpec((comps, PLANES * P2), lambda i: (0, i)),
        ],
        out_specs=main,
        out_shape=jax.ShapeDtypeStruct(start.shape, jnp.float32),
        scratch_shapes=[pltpu.VMEM((PLANES + 2, comps, genes, rows, P2), jnp.float32)],
        compiler_params=pltpu.CompilerParams(vmem_limit_bytes=VMEM_LIMIT),
        cost_estimate=pl.CostEstimate(
            flops=30 * start.size, bytes_accessed=16 * start.size, transcendentals=0
        ),
    )(rates, bound, row_rates, diagonals, columns, start, velocity, start, velocity, start, velocity, halo)


def add_rows(slope, returned, bound, component):
    _, _, rows, cells = slope.shape
    blocks, _, width = returned.shape
    per_step = max(1, min(blocks, 8192 // width))

    def kernel(bound_ref, slope_ref, returned_ref, out_ref):
        step = pl.program_id(0)
        for part in range(per_step):
            cell = (step * per_step + part) * width + lax.broadcasted_iota(
                jnp.int32, (rows, width), 1
            )
            lanes = slice(part * width, (part + 1) * width)
            out_ref[:, lanes] = slope_ref[:, lanes] + jnp.where(
                (cell // P2) < bound_ref[:, 0:1], returned_ref[part], 0.0
            )

    spec = pl.BlockSpec((None, None, rows, per_step * width), lambda j: (component, 1, 0, j))
    return pl.pallas_call(
        kernel,
        grid=(blocks // per_step,),
        in_specs=[
            pl.BlockSpec((rows, 128), lambda j: (0, 0)),
            spec,
            pl.BlockSpec((per_step, rows, width), lambda j: (j, 0, 0)),
        ],
        out_specs=spec,
        out_shape=jax.ShapeDtypeStruct(slope.shape, jnp.float32),
        input_output_aliases={1: 0},
        compiler_params=pltpu.CompilerParams(vmem_limit_bytes=VMEM_LIMIT),
        cost_estimate=pl.CostEstimate(
            flops=2 * rows * cells, bytes_accessed=12 * rows * cells, transcendentals=0
        ),
    )(bound, slope, returned)


def local(
    starting_joint_sensitivities,
    former_section_velocity,
    nominal_coefficient_factors,
    unlocking_coefficients_by_grade,
    repression_grade_by_abundance,
    measured_outbreak_frequencies,
    upper_bounds_per_abundance,
):
    start, velocity = starting_joint_sensitivities, former_section_velocity
    comps, genes, rows, cells = start.shape
    blocks = lax.axis_size("slab")
    width = cells // blocks
    breadth = measured_outbreak_frequencies.shape[0]
    rates = nominal_coefficient_factors * jnp.array(nominal_coefficient_basis, dtype=jnp.float32)
    burst, trans, off, mdecay, decay1, make2, decay2 = [rates[place] for place in range(7)]
    bound = jnp.broadcast_to(upper_bounds_per_abundance[:, None], (rows, 128))

    order = (2, 3, 0, 1)
    arrived = {}
    for comp in order:
        sent = on_state(start, velocity, bound, comp, blocks)
        came = lax.all_to_all(sent, "slab", split_axis=0, concat_axis=0, tiled=True)
        arrived[comp] = came.reshape(breadth, width)

    first_index = jnp.arange(cells, dtype=jnp.int32) // P2
    lowest = start[:, 0, 0, :] + section_step * velocity[:, 0, 0, :]
    lowest = jnp.where(first_index[None, :] < upper_bounds_per_abundance[0], lowest, 0.0)
    halo = shifted(lowest, "slab", -1)

    first_row = lax.axis_index("slab") * rows
    m_count = (first_row + jnp.arange(rows, dtype=jnp.int32)).astype(jnp.float32)
    c_count = jnp.arange(P2, dtype=jnp.float32)
    kon = kon_rates(unlocking_coefficients_by_grade, repression_grade_by_abundance)
    row_rates = jnp.concatenate(
        [
            jnp.broadcast_to((trans * m_count)[:, None], (rows, 128)),
            jnp.broadcast_to((mdecay * (m_count + 1.0))[:, None], (rows, 128)),
        ],
        axis=1,
    )
    shared = -((trans * m_count)[:, None] + (decay2 * c_count)[None, :])
    diagonals = jnp.stack(
        [shared - (mdecay * m_count)[:, None] - kon[None, :], shared - off], axis=0
    )
    columns = jnp.zeros((8, P2), jnp.float32)
    columns = columns.at[0].set(kon)
    columns = columns.at[1].set((c_count >= 1.0).astype(jnp.float32))
    columns = columns.at[2].set(jnp.where(c_count < P2 - 1.0, decay2 * (c_count + 1.0), 0.0))
    slope = partial_slope(start, velocity, halo, rates, bound, row_rates, diagonals, columns)

    unit = jnp.eye(breadth, dtype=jnp.float32)
    m_all = jnp.arange(breadth, dtype=jnp.float32)
    episodes = burst * (episode_share_stencil(measured_outbreak_frequencies, breadth) - unit)
    removal = mdecay * (
        (m_all + 1.0)[:, None] * jnp.eye(breadth, k=1, dtype=jnp.float32) - m_all[:, None] * unit
    )
    matrix = episodes + removal

    returned = {}
    for comp in order:
        total = jnp.dot(matrix, arrived[comp], precision=HIGHEST)
        if comp == 1:
            total = total + jnp.dot(episodes, arrived[0], precision=HIGHEST)
        returned[comp] = lax.all_to_all(
            total.reshape(blocks, rows, width), "slab", split_axis=0, concat_axis=0, tiled=True
        )
    for comp in order:
        slope = add_rows(slope, returned[comp], bound, comp)
    return slope


def solution(mesh):
    placed = (
        P("ens", None, "slab", None),
        P("ens", None, "slab", None),
        P("ens"),
        P("ens"),
        P(),
        P(),
        P("slab"),
    )
    return jax.shard_map(
        local, mesh=mesh, in_specs=placed, out_specs=P("ens", None, "slab", None), check_vma=False
    )
```

```python
import functools

import jax
import jax.numpy as jnp
from jax import lax
from jax.experimental import pallas as pl
from jax.experimental.pallas import tpu as pltpu
from jax.sharding import PartitionSpec as P

P2 = 1024
nominal_coefficient_basis = (2.0, 0.02, 1.0, 0.01, 0.02, 0.03, 0.002)
section_step = 0.125
PLANES = 8
VMEM_LIMIT = 48 * 1024 * 1024
HIGHEST = lax.Precision.HIGHEST


def shifted(value, axis, steps):
    count = lax.axis_size(axis)
    first, last = (max(0, -steps), min(count, count - steps))
    return lax.ppermute(value, axis, [(source, source + steps) for source in range(first, last)])


def episode_share_stencil(measured_outbreak_frequencies, stencil_breadth):
    episode_extents = jnp.arange(stencil_breadth, dtype=jnp.int32)
    episode_shares = measured_outbreak_frequencies.astype(jnp.float32) * (
        episode_extents >= 1
    ).astype(jnp.float32)
    episode_shares = episode_shares / jnp.sum(episode_shares)
    backward_difference = episode_extents[:, None] - episode_extents[None, :]
    single_selector = (backward_difference[:, :, None] == episode_extents[None, None, :]).astype(
        jnp.float32
    )
    return jnp.dot(single_selector, episode_shares, precision=HIGHEST)


def kon_rates(unlocking_coefficients_by_grade, repression_grade_by_abundance):
    levels = jnp.arange(unlocking_coefficients_by_grade.shape[0], dtype=jnp.int32)
    single_selector = (repression_grade_by_abundance[:, None] == levels[None, :]).astype(
        jnp.float32
    )
    return jnp.dot(single_selector, unlocking_coefficients_by_grade, precision=HIGHEST)


def on_state(start, velocity, bound_cells, pair, blocks):
    _, _, rows, cells = start.shape
    width = cells // blocks
    per_step = max(1, min(blocks, 8192 // width))

    def kernel(bound_ref, start_ref, velocity_ref, out_ref):
        step = pl.program_id(0)
        lane = lax.broadcasted_iota(jnp.int32, (rows, width), 1)
        for part in range(per_step):
            lanes = slice(part * width, (part + 1) * width)
            limit = bound_ref[:, 0:1] - (step * per_step + part) * width
            for comp in range(2):
                value = start_ref[comp, :, lanes] + section_step * velocity_ref[comp, :, lanes]
                out_ref[part, :, comp * width : (comp + 1) * width] = jnp.where(
                    lane < limit, value, 0.0
                )

    spec = pl.BlockSpec((2, None, rows, per_step * width), lambda j: (pair, 1, 0, j))
    return pl.pallas_call(
        kernel,
        grid=(blocks // per_step,),
        in_specs=[pl.BlockSpec((rows, 128), lambda j: (0, 0)), spec, spec],
        out_specs=pl.BlockSpec((per_step, rows, 2 * width), lambda j: (j, 0, 0)),
        out_shape=jax.ShapeDtypeStruct((blocks, rows, 2 * width), jnp.float32),
        compiler_params=pltpu.CompilerParams(vmem_limit_bytes=VMEM_LIMIT),
        cost_estimate=pl.CostEstimate(
            flops=6 * rows * cells, bytes_accessed=24 * rows * cells, transcendentals=0
        ),
    )(bound_cells, start, velocity)


def partial_slope(start, velocity, halo, rates, bound, row_rates, diagonals, columns):
    comps, genes, rows, cells = start.shape
    firsts = cells // P2
    steps = firsts // PLANES

    def kernel(
        rate_ref,
        bound_ref,
        row_ref,
        diagonal_ref,
        column_ref,
        start_ref,
        velocity_ref,
        start_low,
        velocity_low,
        start_high,
        velocity_high,
        halo_ref,
        out_ref,
        state,
    ):
        step = pl.program_id(0)
        off, decay1, make2 = rate_ref[2], rate_ref[4], rate_ref[5]
        first_plane = step * PLANES
        bound_column = bound_ref[:, 0:1]

        def masked(plane, value):
            return jnp.where((bound_column > plane) & (plane >= 0), value, 0.0)

        for comp in range(comps):
            for gene in range(genes):
                state[0, comp, gene] = masked(
                    first_plane - 1,
                    start_low[comp, gene] + section_step * velocity_low[comp, gene],
                )
                high = start_high[comp, gene] + section_step * velocity_high[comp, gene]
                state[PLANES + 1, comp, gene] = jnp.where(
                    first_plane + PLANES < firsts, masked(first_plane + PLANES, high), 0.0
                )

        @pl.loop(0, PLANES)
        def _(plane):
            lanes = pl.ds(pl.multiple_of(plane * P2, P2), P2)
            for comp in range(comps):
                for gene in range(genes):
                    state[plane + 1, comp, gene] = masked(
                        first_plane + plane,
                        start_ref[comp, gene, :, lanes]
                        + section_step * velocity_ref[comp, gene, :, lanes],
                    )

        @pl.loop(0, PLANES)
        def _(plane):
            lanes = pl.ds(pl.multiple_of(plane * P2, P2), P2)
            count = (first_plane + plane).astype(jnp.float32)
            inside = bound_column > first_plane + plane
            trans_m = row_ref[:, 0:1]
            mdecay_up = row_ref[:, 128:129]
            own = -count * (decay1 + make2)
            above_rate = decay1 * (count + 1.0)
            made = (make2 * count) * column_ref[1:2, :]
            removed = column_ref[2:3, :]
            kon = column_ref[0:1, :]
            last_row = lax.broadcasted_iota(jnp.int32, (rows, P2), 0) == rows - 1
            for comp in range(comps):
                silent = state[plane + 1, comp, 0]
                active = state[plane + 1, comp, 1]
                for gene in range(genes):
                    value = silent if gene == 0 else active
                    lower = state[plane, comp, gene]
                    total = (diagonal_ref[gene] + own) * value
                    total = total + trans_m * lower
                    total = total + above_rate * state[plane + 2, comp, gene]
                    total = total + made * pltpu.roll(value, 1, 1)
                    total = total + removed * pltpu.roll(value, P2 - 1, 1)
                    if gene == 0:
                        total = total + off * active
                        beyond = jnp.where(
                            last_row,
                            halo_ref[comp : comp + 1, lanes],
                            pltpu.roll(value, rows - 1, 0),
                        )
                        total = total + mdecay_up * beyond
                    else:
                        total = total + kon * silent
                    if comp == 2:
                        total = total + trans_m * (
                            state[plane, 0, gene] - state[plane + 1, 0, gene]
                        )
                    if comp == 3:
                        source = off * state[plane + 1, 0, 1]
                        total = total + source if gene == 0 else total - source
                    out_ref[comp, gene, :, lanes] = jnp.where(inside, total, 0.0)

    def whole(shape):
        return pl.BlockSpec(shape, lambda i: (0,) * len(shape))

    main = pl.BlockSpec((comps, genes, rows, PLANES * P2), lambda i: (0, 0, 0, i))
    low = pl.BlockSpec((comps, genes, rows, P2), lambda i: (0, 0, 0, jnp.maximum(i * PLANES - 1, 0)))
    high = pl.BlockSpec(
        (comps, genes, rows, P2), lambda i: (0, 0, 0, jnp.minimum((i + 1) * PLANES, firsts - 1))
    )
    return pl.pallas_call(
        kernel,
        grid=(steps,),
        in_specs=[
            pl.BlockSpec(memory_space=pltpu.SMEM),
            whole((rows, 128)),
            whole((rows, 256)),
            whole((genes, rows, P2)),
            whole((8, P2)),
            main,
            main,
            low,
            low,
            high,
            high,
            pl.BlockSpec((comps, PLANES * P2), lambda i: (0, i)),
        ],
        out_specs=main,
        out_shape=jax.ShapeDtypeStruct(start.shape, jnp.float32),
        scratch_shapes=[pltpu.VMEM((PLANES + 2, comps, genes, rows, P2), jnp.float32)],
        compiler_params=pltpu.CompilerParams(vmem_limit_bytes=VMEM_LIMIT),
        cost_estimate=pl.CostEstimate(
            flops=30 * start.size, bytes_accessed=16 * start.size, transcendentals=0
        ),
    )(rates, bound, row_rates, diagonals, columns, start, velocity, start, velocity, start, velocity, halo)


def add_rows(slope, returned, bound_cells, pair):
    _, _, rows, cells = slope.shape
    blocks = returned.shape[0]
    width = cells // blocks
    per_step = max(1, min(blocks, 8192 // width))

    def kernel(bound_ref, slope_ref, returned_ref, out_ref):
        step = pl.program_id(0)
        lane = lax.broadcasted_iota(jnp.int32, (rows, width), 1)
        for part in range(per_step):
            lanes = slice(part * width, (part + 1) * width)
            limit = bound_ref[:, 0:1] - (step * per_step + part) * width
            for comp in range(2):
                value = returned_ref[part, :, comp * width : (comp + 1) * width]
                out_ref[comp, :, lanes] = slope_ref[comp, :, lanes] + jnp.where(
                    lane < limit, value, 0.0
                )

    spec = pl.BlockSpec((2, None, rows, per_step * width), lambda j: (pair, 1, 0, j))
    return pl.pallas_call(
        kernel,
        grid=(blocks // per_step,),
        in_specs=[
            pl.BlockSpec((rows, 128), lambda j: (0, 0)),
            spec,
            pl.BlockSpec((per_step, rows, 2 * width), lambda j: (j, 0, 0)),
        ],
        out_specs=spec,
        out_shape=jax.ShapeDtypeStruct(slope.shape, jnp.float32),
        input_output_aliases={1: 0},
        compiler_params=pltpu.CompilerParams(vmem_limit_bytes=VMEM_LIMIT),
        cost_estimate=pl.CostEstimate(
            flops=4 * rows * cells, bytes_accessed=24 * rows * cells, transcendentals=0
        ),
    )(bound_cells, slope, returned)


def local(
    starting_joint_sensitivities,
    former_section_velocity,
    nominal_coefficient_factors,
    unlocking_coefficients_by_grade,
    repression_grade_by_abundance,
    measured_outbreak_frequencies,
    upper_bounds_per_abundance,
):
    start, velocity = starting_joint_sensitivities, former_section_velocity
    comps, genes, rows, cells = start.shape
    blocks = lax.axis_size("slab")
    width = cells // blocks
    breadth = measured_outbreak_frequencies.shape[0]
    rates = nominal_coefficient_factors * jnp.array(nominal_coefficient_basis, dtype=jnp.float32)
    burst, trans, off, mdecay, decay1, make2, decay2 = [rates[place] for place in range(7)]
    bound = jnp.broadcast_to(upper_bounds_per_abundance[:, None], (rows, 128))

    bound_cells = bound * P2

    def exchanged(value):
        return lax.all_to_all(value, "slab", split_axis=0, concat_axis=0, tiled=True)

    first_index = jnp.arange(cells, dtype=jnp.int32) // P2
    lowest = start[:, 0, 0, :] + section_step * velocity[:, 0, 0, :]
    lowest = jnp.where(first_index[None, :] < upper_bounds_per_abundance[0], lowest, 0.0)
    halo = shifted(lowest, "slab", -1)

    came_late = exchanged(on_state(start, velocity, bound_cells, 1, blocks))
    sent_early, halo = lax.optimization_barrier(
        (on_state(start, velocity, bound_cells, 0, blocks), halo)
    )
    came_early = exchanged(sent_early)

    first_row = lax.axis_index("slab") * rows
    m_count = (first_row + jnp.arange(rows, dtype=jnp.int32)).astype(jnp.float32)
    c_count = jnp.arange(P2, dtype=jnp.float32)
    kon = kon_rates(unlocking_coefficients_by_grade, repression_grade_by_abundance)
    row_rates = jnp.concatenate(
        [
            jnp.broadcast_to((trans * m_count)[:, None], (rows, 128)),
            jnp.broadcast_to((mdecay * (m_count + 1.0))[:, None], (rows, 128)),
        ],
        axis=1,
    )
    shared = -((trans * m_count)[:, None] + (decay2 * c_count)[None, :])
    diagonals = jnp.stack(
        [shared - (mdecay * m_count)[:, None] - kon[None, :], shared - off], axis=0
    )
    columns = jnp.zeros((8, P2), jnp.float32)
    columns = columns.at[0].set(kon)
    columns = columns.at[1].set((c_count >= 1.0).astype(jnp.float32))
    columns = columns.at[2].set(jnp.where(c_count < P2 - 1.0, decay2 * (c_count + 1.0), 0.0))
    slope = partial_slope(start, velocity, halo, rates, bound, row_rates, diagonals, columns)

    unit = jnp.eye(breadth, dtype=jnp.float32)
    m_all = jnp.arange(breadth, dtype=jnp.float32)
    episodes = burst * (episode_share_stencil(measured_outbreak_frequencies, breadth) - unit)
    removal = mdecay * (
        (m_all + 1.0)[:, None] * jnp.eye(breadth, k=1, dtype=jnp.float32) - m_all[:, None] * unit
    )
    matrix = episodes + removal

    total_late = jnp.dot(matrix, came_late.reshape(breadth, 2 * width), precision=HIGHEST)
    total_late, slope = lax.optimization_barrier((total_late, slope))
    returned_late = exchanged(total_late.reshape(blocks, rows, 2 * width))
    fields = came_early.reshape(breadth, 2 * width)
    source = jnp.dot(episodes, fields[:, :width], precision=HIGHEST)
    total_early = jnp.dot(matrix, fields, precision=HIGHEST) + jnp.pad(source, ((0, 0), (width, 0)))
    returned_early = exchanged(total_early.reshape(blocks, rows, 2 * width))
    slope = add_rows(slope, returned_late, bound_cells, 1)
    return add_rows(slope, returned_early, bound_cells, 0)


def solution(mesh):
    placed = (
        P("ens", None, "slab", None),
        P("ens", None, "slab", None),
        P("ens"),
        P("ens"),
        P(),
        P(),
        P("slab"),
    )
    return jax.shard_map(
        local, mesh=mesh, in_specs=placed, out_specs=P("ens", None, "slab", None), check_vma=False
    )
```

```python
import functools

import jax
import jax.numpy as jnp
from jax import lax
from jax.experimental import pallas as pl
from jax.experimental.pallas import tpu as pltpu
from jax.sharding import PartitionSpec as P

P2 = 1024
nominal_coefficient_basis = (2.0, 0.02, 1.0, 0.01, 0.02, 0.03, 0.002)
section_step = 0.125
PLANES = 8
VMEM_LIMIT = 48 * 1024 * 1024
HIGHEST = lax.Precision.HIGHEST


def shifted(value, axis, steps):
    count = lax.axis_size(axis)
    first, last = (max(0, -steps), min(count, count - steps))
    return lax.ppermute(value, axis, [(source, source + steps) for source in range(first, last)])


def episode_share_stencil(measured_outbreak_frequencies, stencil_breadth):
    episode_extents = jnp.arange(stencil_breadth, dtype=jnp.int32)
    episode_shares = measured_outbreak_frequencies.astype(jnp.float32) * (
        episode_extents >= 1
    ).astype(jnp.float32)
    episode_shares = episode_shares / jnp.sum(episode_shares)
    backward_difference = episode_extents[:, None] - episode_extents[None, :]
    single_selector = (backward_difference[:, :, None] == episode_extents[None, None, :]).astype(
        jnp.float32
    )
    return jnp.dot(single_selector, episode_shares, precision=HIGHEST)


def kon_rates(unlocking_coefficients_by_grade, repression_grade_by_abundance):
    levels = jnp.arange(unlocking_coefficients_by_grade.shape[0], dtype=jnp.int32)
    single_selector = (repression_grade_by_abundance[:, None] == levels[None, :]).astype(
        jnp.float32
    )
    return jnp.dot(single_selector, unlocking_coefficients_by_grade, precision=HIGHEST)


def on_state(start, velocity, bound_cells, pair, blocks):
    _, _, rows, cells = start.shape
    width = cells // blocks
    per_step = max(1, min(blocks, 8192 // width))

    def kernel(bound_ref, start_ref, velocity_ref, out_ref):
        step = pl.program_id(0)
        lane = lax.broadcasted_iota(jnp.int32, (rows, width), 1)
        for part in range(per_step):
            lanes = slice(part * width, (part + 1) * width)
            limit = bound_ref[:, 0:1] - (step * per_step + part) * width
            for comp in range(2):
                value = start_ref[comp, :, lanes] + section_step * velocity_ref[comp, :, lanes]
                out_ref[part, :, comp * width : (comp + 1) * width] = jnp.where(
                    lane < limit, value, 0.0
                )

    spec = pl.BlockSpec((2, None, rows, per_step * width), lambda j: (pair, 1, 0, j))
    return pl.pallas_call(
        kernel,
        grid=(blocks // per_step,),
        in_specs=[pl.BlockSpec((rows, 128), lambda j: (0, 0)), spec, spec],
        out_specs=pl.BlockSpec((per_step, rows, 2 * width), lambda j: (j, 0, 0)),
        out_shape=jax.ShapeDtypeStruct((blocks, rows, 2 * width), jnp.float32),
        compiler_params=pltpu.CompilerParams(vmem_limit_bytes=VMEM_LIMIT),
        cost_estimate=pl.CostEstimate(
            flops=6 * rows * cells, bytes_accessed=24 * rows * cells, transcendentals=0
        ),
    )(bound_cells, start, velocity)


def partial_slope(start, velocity, halo, rates, bound, row_rates, diagonals, columns):
    comps, genes, rows, cells = start.shape
    firsts = cells // P2
    steps = firsts // PLANES

    def kernel(
        rate_ref,
        bound_ref,
        row_ref,
        diagonal_ref,
        column_ref,
        start_ref,
        velocity_ref,
        start_low,
        velocity_low,
        start_high,
        velocity_high,
        halo_ref,
        out_ref,
        state,
    ):
        step = pl.program_id(0)
        off, decay1, make2 = rate_ref[2], rate_ref[4], rate_ref[5]
        first_plane = step * PLANES
        bound_column = bound_ref[:, 0:1]

        def masked(plane, value):
            return jnp.where((bound_column > plane) & (plane >= 0), value, 0.0)

        for comp in range(comps):
            for gene in range(genes):
                state[0, comp, gene] = masked(
                    first_plane - 1,
                    start_low[comp, gene] + section_step * velocity_low[comp, gene],
                )
                high = start_high[comp, gene] + section_step * velocity_high[comp, gene]
                state[PLANES + 1, comp, gene] = jnp.where(
                    first_plane + PLANES < firsts, masked(first_plane + PLANES, high), 0.0
                )

        @pl.loop(0, PLANES)
        def _(plane):
            lanes = pl.ds(pl.multiple_of(plane * P2, P2), P2)
            for comp in range(comps):
                for gene in range(genes):
                    state[plane + 1, comp, gene] = masked(
                        first_plane + plane,
                        start_ref[comp, gene, :, lanes]
                        + section_step * velocity_ref[comp, gene, :, lanes],
                    )

        @pl.loop(0, PLANES)
        def _(plane):
            lanes = pl.ds(pl.multiple_of(plane * P2, P2), P2)
            count = (first_plane + plane).astype(jnp.float32)
            inside = bound_column > first_plane + plane
            trans_m = row_ref[:, 0:1]
            mdecay_up = row_ref[:, 128:129]
            own = -count * (decay1 + make2)
            above_rate = decay1 * (count + 1.0)
            made = (make2 * count) * column_ref[1:2, :]
            removed = column_ref[2:3, :]
            kon = column_ref[0:1, :]
            last_row = lax.broadcasted_iota(jnp.int32, (rows, P2), 0) == rows - 1
            for comp in range(comps):
                silent = state[plane + 1, comp, 0]
                active = state[plane + 1, comp, 1]
                for gene in range(genes):
                    value = silent if gene == 0 else active
                    lower = state[plane, comp, gene]
                    total = (diagonal_ref[gene] + own) * value
                    total = total + trans_m * lower
                    total = total + above_rate * state[plane + 2, comp, gene]
                    total = total + made * pltpu.roll(value, 1, 1)
                    total = total + removed * pltpu.roll(value, P2 - 1, 1)
                    if gene == 0:
                        total = total + off * active
                        beyond = jnp.where(
                            last_row,
                            halo_ref[comp : comp + 1, lanes],
                            pltpu.roll(value, rows - 1, 0),
                        )
                        total = total + mdecay_up * beyond
                    else:
                        total = total + kon * silent
                    if comp == 2:
                        total = total + trans_m * (
                            state[plane, 0, gene] - state[plane + 1, 0, gene]
                        )
                    if comp == 3:
                        source = off * state[plane + 1, 0, 1]
                        total = total + source if gene == 0 else total - source
                    out_ref[comp, gene, :, lanes] = jnp.where(inside, total, 0.0)

    def whole(shape):
        return pl.BlockSpec(shape, lambda i: (0,) * len(shape))

    main = pl.BlockSpec((comps, genes, rows, PLANES * P2), lambda i: (0, 0, 0, i))
    low = pl.BlockSpec((comps, genes, rows, P2), lambda i: (0, 0, 0, jnp.maximum(i * PLANES - 1, 0)))
    high = pl.BlockSpec(
        (comps, genes, rows, P2), lambda i: (0, 0, 0, jnp.minimum((i + 1) * PLANES, firsts - 1))
    )
    return pl.pallas_call(
        kernel,
        grid=(steps,),
        in_specs=[
            pl.BlockSpec(memory_space=pltpu.SMEM),
            whole((rows, 128)),
            whole((rows, 256)),
            whole((genes, rows, P2)),
            whole((8, P2)),
            main,
            main,
            low,
            low,
            high,
            high,
            pl.BlockSpec((comps, PLANES * P2), lambda i: (0, i)),
        ],
        out_specs=main,
        out_shape=jax.ShapeDtypeStruct(start.shape, jnp.float32),
        scratch_shapes=[pltpu.VMEM((PLANES + 2, comps, genes, rows, P2), jnp.float32)],
        compiler_params=pltpu.CompilerParams(vmem_limit_bytes=VMEM_LIMIT),
        cost_estimate=pl.CostEstimate(
            flops=30 * start.size, bytes_accessed=16 * start.size, transcendentals=0
        ),
    )(rates, bound, row_rates, diagonals, columns, start, velocity, start, velocity, start, velocity, halo)


def add_rows(slope, returned, bound_cells, pair):
    _, _, rows, cells = slope.shape
    blocks = returned.shape[0]
    width = cells // blocks
    per_step = max(1, min(blocks, 8192 // width))

    def kernel(bound_ref, slope_ref, returned_ref, out_ref):
        step = pl.program_id(0)
        lane = lax.broadcasted_iota(jnp.int32, (rows, width), 1)
        for part in range(per_step):
            lanes = slice(part * width, (part + 1) * width)
            limit = bound_ref[:, 0:1] - (step * per_step + part) * width
            for comp in range(2):
                value = returned_ref[part, :, comp * width : (comp + 1) * width]
                out_ref[comp, :, lanes] = slope_ref[comp, :, lanes] + jnp.where(
                    lane < limit, value, 0.0
                )

    spec = pl.BlockSpec((2, None, rows, per_step * width), lambda j: (pair, 1, 0, j))
    return pl.pallas_call(
        kernel,
        grid=(blocks // per_step,),
        in_specs=[
            pl.BlockSpec((rows, 128), lambda j: (0, 0)),
            spec,
            pl.BlockSpec((per_step, rows, 2 * width), lambda j: (j, 0, 0)),
        ],
        out_specs=spec,
        out_shape=jax.ShapeDtypeStruct(slope.shape, jnp.float32),
        input_output_aliases={1: 0},
        compiler_params=pltpu.CompilerParams(vmem_limit_bytes=VMEM_LIMIT),
        cost_estimate=pl.CostEstimate(
            flops=4 * rows * cells, bytes_accessed=24 * rows * cells, transcendentals=0
        ),
    )(bound_cells, slope, returned)


def exchange_rest(matrix, episodes, came_late, sent_early, rows):
    blocks, _, wide = sent_early.shape
    breadth = blocks * rows
    half = wide // 2
    tile = min(512, half)

    def kernel(
        matrix_ref,
        episode_ref,
        late_ref,
        sent_ref,
        late_out,
        early_out,
        fields,
        late_total,
        early_total,
        send_sem,
        recv_sem,
        own_sem,
    ):
        me = lax.axis_index("slab")
        barrier = pltpu.get_barrier_semaphore()

        @pl.loop(1, blocks)
        def _(hop):
            pl.semaphore_signal(
                barrier,
                inc=1,
                device_id={"slab": lax.rem(me + hop, blocks)},
                device_id_type=pl.DeviceIdType.MESH,
            )

        pl.semaphore_wait(barrier, blocks - 1)

        def transfer(phase, source, target, hop):
            peer = lax.rem(me + hop, blocks)
            return pltpu.make_async_remote_copy(
                src_ref=source.at[peer],
                dst_ref=target.at[me],
                send_sem=send_sem.at[phase, hop],
                recv_sem=recv_sem.at[phase, hop],
                device_id={"slab": peer},
                device_id_type=pl.DeviceIdType.MESH,
            )

        def start(phase, source, target):
            @pl.loop(1, blocks)
            def _(hop):
                transfer(phase, source, target, hop).start()

            pltpu.make_async_copy(source.at[me], target.at[me], own_sem.at[phase]).start()

        def arrive(phase, source, target):
            @pl.loop(1, blocks)
            def _(hop):
                transfer(phase, source, target, hop).wait_recv()

            pltpu.make_async_copy(source.at[me], target.at[me], own_sem.at[phase]).wait()

        def leave(phase, source, target):
            @pl.loop(1, blocks)
            def _(hop):
                transfer(phase, source, target, hop).wait_send()

        start(0, sent_ref, fields)

        def product(left, right):
            return jnp.dot(
                left, right.reshape(breadth, tile), precision=HIGHEST,
                preferred_element_type=jnp.float32,
            )

        @pl.loop(0, wide // tile)
        def _(step):
            lanes = pl.ds(pl.multiple_of(step * tile, tile), tile)
            total = product(matrix_ref[...], late_ref[:, :, lanes])
            late_total[:, :, lanes] = total.reshape(blocks, rows, tile)

        start(1, late_total, late_out)
        arrive(0, sent_ref, fields)

        @pl.loop(0, half // tile)
        def _(step):
            lanes = pl.ds(pl.multiple_of(step * tile, tile), tile)
            beyond = pl.ds(pl.multiple_of(half + step * tile, tile), tile)
            first = fields[:, :, lanes]
            total = product(matrix_ref[...], first)
            early_total[:, :, lanes] = total.reshape(blocks, rows, tile)
            total = product(matrix_ref[...], fields[:, :, beyond]) + product(
                episode_ref[...], first
            )
            early_total[:, :, beyond] = total.reshape(blocks, rows, tile)

        start(2, early_total, early_out)
        arrive(1, late_total, late_out)
        arrive(2, early_total, early_out)
        leave(0, sent_ref, fields)
        leave(1, late_total, late_out)
        leave(2, early_total, early_out)

    shape = jax.ShapeDtypeStruct(sent_early.shape, jnp.float32)
    vmem = pl.BlockSpec(memory_space=pltpu.VMEM)
    anywhere = pl.BlockSpec(memory_space=pl.ANY)
    buffer = pltpu.VMEM(sent_early.shape, jnp.float32)
    return pl.pallas_call(
        kernel,
        in_specs=[vmem, vmem, vmem, anywhere],
        out_specs=[anywhere, anywhere],
        out_shape=[shape, shape],
        scratch_shapes=[
            buffer,
            buffer,
            buffer,
            pltpu.SemaphoreType.DMA((3, blocks)),
            pltpu.SemaphoreType.DMA((3, blocks)),
            pltpu.SemaphoreType.DMA((3,)),
        ],
        compiler_params=pltpu.CompilerParams(
            collective_id=0, has_side_effects=True, vmem_limit_bytes=VMEM_LIMIT
        ),
        cost_estimate=pl.CostEstimate(
            flops=6 * breadth * breadth * wide,
            bytes_accessed=24 * breadth * wide,
            transcendentals=0,
        ),
    )(matrix, episodes, came_late, sent_early)


def local(
    starting_joint_sensitivities,
    former_section_velocity,
    nominal_coefficient_factors,
    unlocking_coefficients_by_grade,
    repression_grade_by_abundance,
    measured_outbreak_frequencies,
    upper_bounds_per_abundance,
):
    start, velocity = starting_joint_sensitivities, former_section_velocity
    comps, genes, rows, cells = start.shape
    blocks = lax.axis_size("slab")
    width = cells // blocks
    breadth = measured_outbreak_frequencies.shape[0]
    rates = nominal_coefficient_factors * jnp.array(nominal_coefficient_basis, dtype=jnp.float32)
    burst, trans, off, mdecay, decay1, make2, decay2 = [rates[place] for place in range(7)]
    bound = jnp.broadcast_to(upper_bounds_per_abundance[:, None], (rows, 128))

    bound_cells = bound * P2

    def exchanged(value):
        return lax.all_to_all(value, "slab", split_axis=0, concat_axis=0, tiled=True)

    first_index = jnp.arange(cells, dtype=jnp.int32) // P2
    lowest = start[:, 0, 0, :] + section_step * velocity[:, 0, 0, :]
    lowest = jnp.where(first_index[None, :] < upper_bounds_per_abundance[0], lowest, 0.0)
    halo = shifted(lowest, "slab", -1)

    came_late = exchanged(on_state(start, velocity, bound_cells, 1, blocks))
    sent_early = on_state(start, velocity, bound_cells, 0, blocks)

    first_row = lax.axis_index("slab") * rows
    m_count = (first_row + jnp.arange(rows, dtype=jnp.int32)).astype(jnp.float32)
    c_count = jnp.arange(P2, dtype=jnp.float32)
    kon = kon_rates(unlocking_coefficients_by_grade, repression_grade_by_abundance)
    row_rates = jnp.concatenate(
        [
            jnp.broadcast_to((trans * m_count)[:, None], (rows, 128)),
            jnp.broadcast_to((mdecay * (m_count + 1.0))[:, None], (rows, 128)),
        ],
        axis=1,
    )
    shared = -((trans * m_count)[:, None] + (decay2 * c_count)[None, :])
    diagonals = jnp.stack(
        [shared - (mdecay * m_count)[:, None] - kon[None, :], shared - off], axis=0
    )
    columns = jnp.zeros((8, P2), jnp.float32)
    columns = columns.at[0].set(kon)
    columns = columns.at[1].set((c_count >= 1.0).astype(jnp.float32))
    columns = columns.at[2].set(jnp.where(c_count < P2 - 1.0, decay2 * (c_count + 1.0), 0.0))
    slope = partial_slope(start, velocity, halo, rates, bound, row_rates, diagonals, columns)

    unit = jnp.eye(breadth, dtype=jnp.float32)
    m_all = jnp.arange(breadth, dtype=jnp.float32)
    episodes = burst * (episode_share_stencil(measured_outbreak_frequencies, breadth) - unit)
    removal = mdecay * (
        (m_all + 1.0)[:, None] * jnp.eye(breadth, k=1, dtype=jnp.float32) - m_all[:, None] * unit
    )
    matrix = episodes + removal

    came_late, sent_early, slope = lax.optimization_barrier((came_late, sent_early, slope))
    returned_late, returned_early = exchange_rest(matrix, episodes, came_late, sent_early, rows)
    slope = add_rows(slope, returned_late, bound_cells, 1)
    return add_rows(slope, returned_early, bound_cells, 0)


def solution(mesh):
    placed = (
        P("ens", None, "slab", None),
        P("ens", None, "slab", None),
        P("ens"),
        P("ens"),
        P(),
        P(),
        P("slab"),
    )
    return jax.shard_map(
        local, mesh=mesh, in_specs=placed, out_specs=P("ens", None, "slab", None), check_vma=False
    )
```

```python
import functools

import jax
import jax.numpy as jnp
from jax import lax
from jax.experimental import pallas as pl
from jax.experimental.pallas import tpu as pltpu
from jax.sharding import PartitionSpec as P

P2 = 1024
nominal_coefficient_basis = (2.0, 0.02, 1.0, 0.01, 0.02, 0.03, 0.002)
section_step = 0.125
PLANES = 8
VMEM_LIMIT = 48 * 1024 * 1024
HIGHEST = lax.Precision.HIGHEST


def shifted(value, axis, steps):
    count = lax.axis_size(axis)
    first, last = (max(0, -steps), min(count, count - steps))
    return lax.ppermute(value, axis, [(source, source + steps) for source in range(first, last)])


def episode_share_stencil(measured_outbreak_frequencies, stencil_breadth):
    episode_extents = jnp.arange(stencil_breadth, dtype=jnp.int32)
    episode_shares = measured_outbreak_frequencies.astype(jnp.float32) * (
        episode_extents >= 1
    ).astype(jnp.float32)
    episode_shares = episode_shares / jnp.sum(episode_shares)
    backward_difference = episode_extents[:, None] - episode_extents[None, :]
    single_selector = (backward_difference[:, :, None] == episode_extents[None, None, :]).astype(
        jnp.float32
    )
    return jnp.dot(single_selector, episode_shares, precision=HIGHEST)


def kon_rates(unlocking_coefficients_by_grade, repression_grade_by_abundance):
    levels = jnp.arange(unlocking_coefficients_by_grade.shape[0], dtype=jnp.int32)
    single_selector = (repression_grade_by_abundance[:, None] == levels[None, :]).astype(
        jnp.float32
    )
    return jnp.dot(single_selector, unlocking_coefficients_by_grade, precision=HIGHEST)


def on_state(start, velocity, bound_cells, pair, blocks):
    _, _, rows, cells = start.shape
    width = cells // blocks
    per_step = max(1, min(blocks, 8192 // width))

    def kernel(bound_ref, start_ref, velocity_ref, out_ref):
        step = pl.program_id(0)
        lane = lax.broadcasted_iota(jnp.int32, (rows, width), 1)
        for part in range(per_step):
            lanes = slice(part * width, (part + 1) * width)
            limit = bound_ref[:, 0:1] - (step * per_step + part) * width
            for comp in range(2):
                value = start_ref[comp, :, lanes] + section_step * velocity_ref[comp, :, lanes]
                out_ref[part, :, comp * width : (comp + 1) * width] = jnp.where(
                    lane < limit, value, 0.0
                )

    spec = pl.BlockSpec((2, None, rows, per_step * width), lambda j: (pair, 1, 0, j))
    return pl.pallas_call(
        kernel,
        grid=(blocks // per_step,),
        in_specs=[pl.BlockSpec((rows, 128), lambda j: (0, 0)), spec, spec],
        out_specs=pl.BlockSpec((per_step, rows, 2 * width), lambda j: (j, 0, 0)),
        out_shape=jax.ShapeDtypeStruct((blocks, rows, 2 * width), jnp.float32),
        compiler_params=pltpu.CompilerParams(vmem_limit_bytes=VMEM_LIMIT),
        cost_estimate=pl.CostEstimate(
            flops=6 * rows * cells, bytes_accessed=24 * rows * cells, transcendentals=0
        ),
    )(bound_cells, start, velocity)


def partial_slope(start, velocity, halo, rates, bound, row_rates, diagonals, columns):
    comps, genes, rows, cells = start.shape
    firsts = cells // P2
    steps = firsts // PLANES

    def kernel(
        rate_ref,
        bound_ref,
        row_ref,
        diagonal_ref,
        column_ref,
        start_ref,
        velocity_ref,
        start_low,
        velocity_low,
        start_high,
        velocity_high,
        halo_ref,
        out_ref,
        state,
    ):
        step = pl.program_id(0)
        off, decay1, make2 = rate_ref[2], rate_ref[4], rate_ref[5]
        first_plane = step * PLANES
        bound_column = bound_ref[:, 0:1]

        def masked(plane, value):
            return jnp.where((bound_column > plane) & (plane >= 0), value, 0.0)

        for comp in range(comps):
            for gene in range(genes):
                state[0, comp, gene] = masked(
                    first_plane - 1,
                    start_low[comp, gene] + section_step * velocity_low[comp, gene],
                )
                high = start_high[comp, gene] + section_step * velocity_high[comp, gene]
                state[PLANES + 1, comp, gene] = jnp.where(
                    first_plane + PLANES < firsts, masked(first_plane + PLANES, high), 0.0
                )

        @pl.loop(0, PLANES)
        def _(plane):
            lanes = pl.ds(pl.multiple_of(plane * P2, P2), P2)
            for comp in range(comps):
                for gene in range(genes):
                    state[plane + 1, comp, gene] = masked(
                        first_plane + plane,
                        start_ref[comp, gene, :, lanes]
                        + section_step * velocity_ref[comp, gene, :, lanes],
                    )

        @pl.loop(0, PLANES)
        def _(plane):
            lanes = pl.ds(pl.multiple_of(plane * P2, P2), P2)
            count = (first_plane + plane).astype(jnp.float32)
            inside = bound_column > first_plane + plane
            trans_m = row_ref[:, 0:1]
            mdecay_up = row_ref[:, 128:129]
            own = -count * (decay1 + make2)
            above_rate = decay1 * (count + 1.0)
            made = (make2 * count) * column_ref[1:2, :]
            removed = column_ref[2:3, :]
            kon = column_ref[0:1, :]
            last_row = lax.broadcasted_iota(jnp.int32, (rows, P2), 0) == rows - 1
            for comp in range(comps):
                silent = state[plane + 1, comp, 0]
                active = state[plane + 1, comp, 1]
                for gene in range(genes):
                    value = silent if gene == 0 else active
                    lower = state[plane, comp, gene]
                    total = (diagonal_ref[gene] + own) * value
                    total = total + trans_m * lower
                    total = total + above_rate * state[plane + 2, comp, gene]
                    total = total + made * pltpu.roll(value, 1, 1)
                    total = total + removed * pltpu.roll(value, P2 - 1, 1)
                    if gene == 0:
                        total = total + off * active
                        beyond = jnp.where(
                            last_row,
                            halo_ref[comp : comp + 1, lanes],
                            pltpu.roll(value, rows - 1, 0),
                        )
                        total = total + mdecay_up * beyond
                    else:
                        total = total + kon * silent
                    if comp == 2:
                        total = total + trans_m * (
                            state[plane, 0, gene] - state[plane + 1, 0, gene]
                        )
                    if comp == 3:
                        source = off * state[plane + 1, 0, 1]
                        total = total + source if gene == 0 else total - source
                    out_ref[comp, gene, :, lanes] = jnp.where(inside, total, 0.0)

    def whole(shape):
        return pl.BlockSpec(shape, lambda i: (0,) * len(shape))

    main = pl.BlockSpec((comps, genes, rows, PLANES * P2), lambda i: (0, 0, 0, i))
    low = pl.BlockSpec((comps, genes, rows, P2), lambda i: (0, 0, 0, jnp.maximum(i * PLANES - 1, 0)))
    high = pl.BlockSpec(
        (comps, genes, rows, P2), lambda i: (0, 0, 0, jnp.minimum((i + 1) * PLANES, firsts - 1))
    )
    return pl.pallas_call(
        kernel,
        grid=(steps,),
        in_specs=[
            pl.BlockSpec(memory_space=pltpu.SMEM),
            whole((rows, 128)),
            whole((rows, 256)),
            whole((genes, rows, P2)),
            whole((8, P2)),
            main,
            main,
            low,
            low,
            high,
            high,
            pl.BlockSpec((comps, PLANES * P2), lambda i: (0, i)),
        ],
        out_specs=main,
        out_shape=jax.ShapeDtypeStruct(start.shape, jnp.float32),
        scratch_shapes=[pltpu.VMEM((PLANES + 2, comps, genes, rows, P2), jnp.float32)],
        compiler_params=pltpu.CompilerParams(vmem_limit_bytes=VMEM_LIMIT),
        cost_estimate=pl.CostEstimate(
            flops=30 * start.size, bytes_accessed=16 * start.size, transcendentals=0
        ),
    )(rates, bound, row_rates, diagonals, columns, start, velocity, start, velocity, start, velocity, halo)


def add_rows(slope, early, late, bound_cells):
    comps, _, rows, cells = slope.shape
    blocks = early.shape[0]
    width = cells // blocks
    per_step = max(1, min(blocks, 8192 // width))

    def kernel(bound_ref, slope_ref, early_ref, late_ref, out_ref):
        step = pl.program_id(0)
        lane = lax.broadcasted_iota(jnp.int32, (rows, width), 1)
        for part in range(per_step):
            lanes = slice(part * width, (part + 1) * width)
            limit = bound_ref[:, 0:1] - (step * per_step + part) * width
            for comp in range(comps):
                source = early_ref if comp < 2 else late_ref
                place = (comp % 2) * width
                value = source[part, :, place : place + width]
                out_ref[comp, :, lanes] = slope_ref[comp, :, lanes] + jnp.where(
                    lane < limit, value, 0.0
                )

    spec = pl.BlockSpec((comps, None, rows, per_step * width), lambda j: (0, 1, 0, j))
    pair = pl.BlockSpec((per_step, rows, 2 * width), lambda j: (j, 0, 0))
    return pl.pallas_call(
        kernel,
        grid=(blocks // per_step,),
        in_specs=[pl.BlockSpec((rows, 128), lambda j: (0, 0)), spec, pair, pair],
        out_specs=spec,
        out_shape=jax.ShapeDtypeStruct(slope.shape, jnp.float32),
        input_output_aliases={1: 0},
        compiler_params=pltpu.CompilerParams(vmem_limit_bytes=VMEM_LIMIT),
        cost_estimate=pl.CostEstimate(
            flops=8 * rows * cells, bytes_accessed=48 * rows * cells, transcendentals=0
        ),
    )(bound_cells, slope, early, late)


def exchange_rest(matrix, episodes, came_late, sent_early, rows):
    blocks, _, wide = sent_early.shape
    breadth = blocks * rows
    half = wide // 2
    tile = min(512, half)

    def kernel(
        matrix_ref,
        episode_ref,
        late_ref,
        sent_ref,
        late_out,
        early_out,
        fields,
        late_total,
        early_total,
        send_sem,
        recv_sem,
        own_sem,
    ):
        me = lax.axis_index("slab")
        barrier = pltpu.get_barrier_semaphore()

        @pl.loop(1, blocks)
        def _(hop):
            pl.semaphore_signal(
                barrier,
                inc=1,
                device_id={"slab": lax.rem(me + hop, blocks)},
                device_id_type=pl.DeviceIdType.MESH,
            )

        pl.semaphore_wait(barrier, blocks - 1)

        def transfer(phase, source, target, hop):
            peer = lax.rem(me + hop, blocks)
            return pltpu.make_async_remote_copy(
                src_ref=source.at[peer],
                dst_ref=target.at[me],
                send_sem=send_sem.at[phase, hop],
                recv_sem=recv_sem.at[phase, hop],
                device_id={"slab": peer},
                device_id_type=pl.DeviceIdType.MESH,
            )

        def start(phase, source, target):
            @pl.loop(1, blocks)
            def _(hop):
                transfer(phase, source, target, hop).start()

            pltpu.make_async_copy(source.at[me], target.at[me], own_sem.at[phase]).start()

        def arrive(phase, source, target):
            @pl.loop(1, blocks)
            def _(hop):
                transfer(phase, source, target, hop).wait_recv()

            pltpu.make_async_copy(source.at[me], target.at[me], own_sem.at[phase]).wait()

        def leave(phase, source, target):
            @pl.loop(1, blocks)
            def _(hop):
                transfer(phase, source, target, hop).wait_send()

        start(0, sent_ref, fields)

        def product(left, right):
            return jnp.dot(
                left, right.reshape(breadth, tile), precision=HIGHEST,
                preferred_element_type=jnp.float32,
            )

        @pl.loop(0, wide // tile)
        def _(step):
            lanes = pl.ds(pl.multiple_of(step * tile, tile), tile)
            total = product(matrix_ref[...], late_ref[:, :, lanes])
            late_total[:, :, lanes] = total.reshape(blocks, rows, tile)

        start(1, late_total, late_out)
        arrive(0, sent_ref, fields)

        @pl.loop(0, half // tile)
        def _(step):
            lanes = pl.ds(pl.multiple_of(step * tile, tile), tile)
            beyond = pl.ds(pl.multiple_of(half + step * tile, tile), tile)
            first = fields[:, :, lanes]
            total = product(matrix_ref[...], first)
            early_total[:, :, lanes] = total.reshape(blocks, rows, tile)
            total = product(matrix_ref[...], fields[:, :, beyond]) + product(
                episode_ref[...], first
            )
            early_total[:, :, beyond] = total.reshape(blocks, rows, tile)

        start(2, early_total, early_out)
        arrive(1, late_total, late_out)
        arrive(2, early_total, early_out)
        leave(0, sent_ref, fields)
        leave(1, late_total, late_out)
        leave(2, early_total, early_out)

    shape = jax.ShapeDtypeStruct(sent_early.shape, jnp.float32)
    vmem = pl.BlockSpec(memory_space=pltpu.VMEM)
    anywhere = pl.BlockSpec(memory_space=pl.ANY)
    buffer = pltpu.VMEM(sent_early.shape, jnp.float32)
    return pl.pallas_call(
        kernel,
        in_specs=[vmem, vmem, vmem, anywhere],
        out_specs=[anywhere, anywhere],
        out_shape=[shape, shape],
        scratch_shapes=[
            buffer,
            buffer,
            buffer,
            pltpu.SemaphoreType.DMA((3, blocks)),
            pltpu.SemaphoreType.DMA((3, blocks)),
            pltpu.SemaphoreType.DMA((3,)),
        ],
        compiler_params=pltpu.CompilerParams(
            collective_id=0, has_side_effects=True, vmem_limit_bytes=VMEM_LIMIT
        ),
        cost_estimate=pl.CostEstimate(
            flops=6 * breadth * breadth * wide,
            bytes_accessed=24 * breadth * wide,
            transcendentals=0,
        ),
    )(matrix, episodes, came_late, sent_early)


def local(
    starting_joint_sensitivities,
    former_section_velocity,
    nominal_coefficient_factors,
    unlocking_coefficients_by_grade,
    repression_grade_by_abundance,
    measured_outbreak_frequencies,
    upper_bounds_per_abundance,
):
    start, velocity = starting_joint_sensitivities, former_section_velocity
    comps, genes, rows, cells = start.shape
    blocks = lax.axis_size("slab")
    width = cells // blocks
    breadth = measured_outbreak_frequencies.shape[0]
    rates = nominal_coefficient_factors * jnp.array(nominal_coefficient_basis, dtype=jnp.float32)
    burst, trans, off, mdecay, decay1, make2, decay2 = [rates[place] for place in range(7)]
    bound = jnp.broadcast_to(upper_bounds_per_abundance[:, None], (rows, 128))

    bound_cells = bound * P2

    def exchanged(value):
        return lax.all_to_all(value, "slab", split_axis=0, concat_axis=0, tiled=True)

    first_index = jnp.arange(cells, dtype=jnp.int32) // P2
    lowest = start[:, 0, 0, :] + section_step * velocity[:, 0, 0, :]
    lowest = jnp.where(first_index[None, :] < upper_bounds_per_abundance[0], lowest, 0.0)
    lowest, bound_first = lax.optimization_barrier((lowest, bound_cells))
    halo = shifted(lowest, "slab", -1)
    came_late = exchanged(on_state(start, velocity, bound_first, 1, blocks))
    sent_early = on_state(start, velocity, bound_cells, 0, blocks)

    first_row = lax.axis_index("slab") * rows
    m_count = (first_row + jnp.arange(rows, dtype=jnp.int32)).astype(jnp.float32)
    c_count = jnp.arange(P2, dtype=jnp.float32)
    kon = kon_rates(unlocking_coefficients_by_grade, repression_grade_by_abundance)
    row_rates = jnp.concatenate(
        [
            jnp.broadcast_to((trans * m_count)[:, None], (rows, 128)),
            jnp.broadcast_to((mdecay * (m_count + 1.0))[:, None], (rows, 128)),
        ],
        axis=1,
    )
    shared = -((trans * m_count)[:, None] + (decay2 * c_count)[None, :])
    diagonals = jnp.stack(
        [shared - (mdecay * m_count)[:, None] - kon[None, :], shared - off], axis=0
    )
    columns = jnp.zeros((8, P2), jnp.float32)
    columns = columns.at[0].set(kon)
    columns = columns.at[1].set((c_count >= 1.0).astype(jnp.float32))
    columns = columns.at[2].set(jnp.where(c_count < P2 - 1.0, decay2 * (c_count + 1.0), 0.0))
    slope = partial_slope(start, velocity, halo, rates, bound, row_rates, diagonals, columns)

    unit = jnp.eye(breadth, dtype=jnp.float32)
    m_all = jnp.arange(breadth, dtype=jnp.float32)
    episodes = burst * (episode_share_stencil(measured_outbreak_frequencies, breadth) - unit)
    removal = mdecay * (
        (m_all + 1.0)[:, None] * jnp.eye(breadth, k=1, dtype=jnp.float32) - m_all[:, None] * unit
    )
    matrix = episodes + removal

    came_late, sent_early, slope = lax.optimization_barrier((came_late, sent_early, slope))
    returned_late, returned_early = exchange_rest(matrix, episodes, came_late, sent_early, rows)
    return add_rows(slope, returned_early, returned_late, bound_cells)


def solution(mesh):
    placed = (
        P("ens", None, "slab", None),
        P("ens", None, "slab", None),
        P("ens"),
        P("ens"),
        P(),
        P(),
        P("slab"),
    )
    return jax.shard_map(
        local, mesh=mesh, in_specs=placed, out_specs=P("ens", None, "slab", None), check_vma=False
    )
```

```python
import functools

import jax
import jax.numpy as jnp
from jax import lax
from jax.experimental import pallas as pl
from jax.experimental.pallas import tpu as pltpu
from jax.sharding import PartitionSpec as P

P2 = 1024
nominal_coefficient_basis = (2.0, 0.02, 1.0, 0.01, 0.02, 0.03, 0.002)
section_step = 0.125
PLANES = 8
VMEM_LIMIT = 48 * 1024 * 1024
HIGHEST = lax.Precision.HIGHEST


def shifted(value, axis, steps):
    count = lax.axis_size(axis)
    first, last = (max(0, -steps), min(count, count - steps))
    return lax.ppermute(value, axis, [(source, source + steps) for source in range(first, last)])


def episode_share_stencil(measured_outbreak_frequencies, stencil_breadth):
    episode_extents = jnp.arange(stencil_breadth, dtype=jnp.int32)
    episode_shares = measured_outbreak_frequencies.astype(jnp.float32) * (
        episode_extents >= 1
    ).astype(jnp.float32)
    episode_shares = episode_shares / jnp.sum(episode_shares)
    backward_difference = episode_extents[:, None] - episode_extents[None, :]
    single_selector = (backward_difference[:, :, None] == episode_extents[None, None, :]).astype(
        jnp.float32
    )
    return jnp.dot(single_selector, episode_shares, precision=HIGHEST)


def kon_rates(unlocking_coefficients_by_grade, repression_grade_by_abundance):
    levels = jnp.arange(unlocking_coefficients_by_grade.shape[0], dtype=jnp.int32)
    single_selector = (repression_grade_by_abundance[:, None] == levels[None, :]).astype(
        jnp.float32
    )
    return jnp.dot(single_selector, unlocking_coefficients_by_grade, precision=HIGHEST)


def on_state(start, velocity, bound_cells, pair, blocks):
    _, _, rows, cells = start.shape
    width = cells // blocks
    per_step = max(1, min(blocks, 8192 // width))

    def kernel(bound_ref, start_ref, velocity_ref, out_ref):
        step = pl.program_id(0)
        lane = lax.broadcasted_iota(jnp.int32, (rows, width), 1)
        for part in range(per_step):
            lanes = slice(part * width, (part + 1) * width)
            limit = bound_ref[:, 0:1] - (step * per_step + part) * width
            for comp in range(2):
                value = start_ref[comp, :, lanes] + section_step * velocity_ref[comp, :, lanes]
                out_ref[part, :, comp * width : (comp + 1) * width] = jnp.where(
                    lane < limit, value, 0.0
                )

    spec = pl.BlockSpec((2, None, rows, per_step * width), lambda j: (pair, 1, 0, j))
    return pl.pallas_call(
        kernel,
        grid=(blocks // per_step,),
        in_specs=[pl.BlockSpec((rows, 128), lambda j: (0, 0)), spec, spec],
        out_specs=pl.BlockSpec((per_step, rows, 2 * width), lambda j: (j, 0, 0)),
        out_shape=jax.ShapeDtypeStruct((blocks, rows, 2 * width), jnp.float32),
        compiler_params=pltpu.CompilerParams(vmem_limit_bytes=VMEM_LIMIT),
        cost_estimate=pl.CostEstimate(
            flops=6 * rows * cells, bytes_accessed=24 * rows * cells, transcendentals=0
        ),
    )(bound_cells, start, velocity)


def partial_slope(start, velocity, halo, rates, bound, row_rates, diagonals, columns):
    comps, genes, rows, cells = start.shape
    firsts = cells // P2
    steps = firsts // PLANES

    def kernel(
        rate_ref,
        bound_ref,
        row_ref,
        diagonal_ref,
        column_ref,
        start_ref,
        velocity_ref,
        start_low,
        velocity_low,
        start_high,
        velocity_high,
        halo_ref,
        out_ref,
        state,
    ):
        step = pl.program_id(0)
        off, decay1, make2 = rate_ref[2], rate_ref[4], rate_ref[5]
        first_plane = step * PLANES
        bound_column = bound_ref[:, 0:1]

        def masked(plane, value):
            return jnp.where((bound_column > plane) & (plane >= 0), value, 0.0)

        for comp in range(comps):
            for gene in range(genes):
                state[0, comp, gene] = masked(
                    first_plane - 1,
                    start_low[comp, gene] + section_step * velocity_low[comp, gene],
                )
                high = start_high[comp, gene] + section_step * velocity_high[comp, gene]
                state[PLANES + 1, comp, gene] = jnp.where(
                    first_plane + PLANES < firsts, masked(first_plane + PLANES, high), 0.0
                )

        @pl.loop(0, PLANES)
        def _(plane):
            lanes = pl.ds(pl.multiple_of(plane * P2, P2), P2)
            for comp in range(comps):
                for gene in range(genes):
                    state[plane + 1, comp, gene] = masked(
                        first_plane + plane,
                        start_ref[comp, gene, :, lanes]
                        + section_step * velocity_ref[comp, gene, :, lanes],
                    )

        @pl.loop(0, PLANES)
        def _(plane):
            lanes = pl.ds(pl.multiple_of(plane * P2, P2), P2)
            count = (first_plane + plane).astype(jnp.float32)
            inside = bound_column > first_plane + plane
            trans_m = row_ref[:, 0:1]
            mdecay_up = row_ref[:, 128:129]
            own = -count * (decay1 + make2)
            above_rate = decay1 * (count + 1.0)
            made = (make2 * count) * column_ref[1:2, :]
            removed = column_ref[2:3, :]
            kon = column_ref[0:1, :]
            last_row = lax.broadcasted_iota(jnp.int32, (rows, P2), 0) == rows - 1
            for comp in range(comps):
                silent = state[plane + 1, comp, 0]
                active = state[plane + 1, comp, 1]
                for gene in range(genes):
                    value = silent if gene == 0 else active
                    lower = state[plane, comp, gene]
                    total = (diagonal_ref[gene] + own) * value
                    total = total + trans_m * lower
                    total = total + above_rate * state[plane + 2, comp, gene]
                    total = total + made * pltpu.roll(value, 1, 1)
                    total = total + removed * pltpu.roll(value, P2 - 1, 1)
                    if gene == 0:
                        total = total + off * active
                        beyond = jnp.where(
                            last_row,
                            halo_ref[comp : comp + 1, lanes],
                            pltpu.roll(value, rows - 1, 0),
                        )
                        total = total + mdecay_up * beyond
                    else:
                        total = total + kon * silent
                    if comp == 2:
                        total = total + trans_m * (
                            state[plane, 0, gene] - state[plane + 1, 0, gene]
                        )
                    if comp == 3:
                        source = off * state[plane + 1, 0, 1]
                        total = total + source if gene == 0 else total - source
                    out_ref[comp, gene, :, lanes] = jnp.where(inside, total, 0.0)

    def whole(shape):
        return pl.BlockSpec(shape, lambda i: (0,) * len(shape))

    main = pl.BlockSpec((comps, genes, rows, PLANES * P2), lambda i: (0, 0, 0, i))
    low = pl.BlockSpec((comps, genes, rows, P2), lambda i: (0, 0, 0, jnp.maximum(i * PLANES - 1, 0)))
    high = pl.BlockSpec(
        (comps, genes, rows, P2), lambda i: (0, 0, 0, jnp.minimum((i + 1) * PLANES, firsts - 1))
    )
    return pl.pallas_call(
        kernel,
        grid=(steps,),
        in_specs=[
            pl.BlockSpec(memory_space=pltpu.SMEM),
            whole((rows, 128)),
            whole((rows, 256)),
            whole((genes, rows, P2)),
            whole((8, P2)),
            main,
            main,
            low,
            low,
            high,
            high,
            pl.BlockSpec((comps, PLANES * P2), lambda i: (0, i)),
        ],
        out_specs=main,
        out_shape=jax.ShapeDtypeStruct(start.shape, jnp.float32),
        scratch_shapes=[pltpu.VMEM((PLANES + 2, comps, genes, rows, P2), jnp.float32)],
        compiler_params=pltpu.CompilerParams(vmem_limit_bytes=VMEM_LIMIT),
        cost_estimate=pl.CostEstimate(
            flops=30 * start.size, bytes_accessed=16 * start.size, transcendentals=0
        ),
    )(rates, bound, row_rates, diagonals, columns, start, velocity, start, velocity, start, velocity, halo)


def add_rows(slope, early, late, bound_cells):
    comps, _, rows, cells = slope.shape
    blocks = early.shape[0]
    width = cells // blocks
    per_step = max(1, min(blocks, 8192 // width))

    def kernel(bound_ref, slope_ref, early_ref, late_ref, out_ref):
        step = pl.program_id(0)
        lane = lax.broadcasted_iota(jnp.int32, (rows, width), 1)
        for part in range(per_step):
            lanes = slice(part * width, (part + 1) * width)
            limit = bound_ref[:, 0:1] - (step * per_step + part) * width
            for comp in range(comps):
                source = early_ref if comp < 2 else late_ref
                place = (comp % 2) * width
                value = source[part, :, place : place + width]
                out_ref[comp, :, lanes] = slope_ref[comp, :, lanes] + jnp.where(
                    lane < limit, value, 0.0
                )

    spec = pl.BlockSpec((comps, None, rows, per_step * width), lambda j: (0, 1, 0, j))
    pair = pl.BlockSpec((per_step, rows, 2 * width), lambda j: (j, 0, 0))
    return pl.pallas_call(
        kernel,
        grid=(blocks // per_step,),
        in_specs=[pl.BlockSpec((rows, 128), lambda j: (0, 0)), spec, pair, pair],
        out_specs=spec,
        out_shape=jax.ShapeDtypeStruct(slope.shape, jnp.float32),
        input_output_aliases={1: 0},
        compiler_params=pltpu.CompilerParams(vmem_limit_bytes=VMEM_LIMIT),
        cost_estimate=pl.CostEstimate(
            flops=8 * rows * cells, bytes_accessed=48 * rows * cells, transcendentals=0
        ),
    )(bound_cells, slope, early, late)


def exchange_rest(matrix, episodes, came_late, sent_early, rows):
    blocks, _, wide = sent_early.shape
    breadth = blocks * rows
    half = wide // 2
    tile = min(512, half)

    def kernel(
        matrix_ref,
        episode_ref,
        late_ref,
        sent_ref,
        late_out,
        early_out,
        fields,
        late_total,
        early_total,
        send_sem,
        recv_sem,
        own_sem,
    ):
        me = lax.axis_index("slab")
        barrier = pltpu.get_barrier_semaphore()

        @pl.loop(1, blocks)
        def _(hop):
            pl.semaphore_signal(
                barrier,
                inc=1,
                device_id={"slab": lax.rem(me + hop, blocks)},
                device_id_type=pl.DeviceIdType.MESH,
            )

        pl.semaphore_wait(barrier, blocks - 1)

        def transfer(phase, source, target, hop):
            peer = lax.rem(me + hop, blocks)
            return pltpu.make_async_remote_copy(
                src_ref=source.at[peer],
                dst_ref=target.at[me],
                send_sem=send_sem.at[phase, hop],
                recv_sem=recv_sem.at[phase, hop],
                device_id={"slab": peer},
                device_id_type=pl.DeviceIdType.MESH,
            )

        def start(phase, source, target):
            @pl.loop(1, blocks)
            def _(hop):
                transfer(phase, source, target, hop).start()

            pltpu.make_async_copy(source.at[me], target.at[me], own_sem.at[phase]).start()

        def arrive(phase, source, target):
            @pl.loop(1, blocks)
            def _(hop):
                transfer(phase, source, target, hop).wait_recv()

            pltpu.make_async_copy(source.at[me], target.at[me], own_sem.at[phase]).wait()

        def leave(phase, source, target):
            @pl.loop(1, blocks)
            def _(hop):
                transfer(phase, source, target, hop).wait_send()

        start(0, sent_ref, fields)

        def product(left, right):
            return jnp.dot(
                left, right.reshape(breadth, tile), precision=HIGHEST,
                preferred_element_type=jnp.float32,
            )

        @pl.loop(0, wide // tile)
        def _(step):
            lanes = pl.ds(pl.multiple_of(step * tile, tile), tile)
            total = product(matrix_ref[...], late_ref[:, :, lanes])
            late_total[:, :, lanes] = total.reshape(blocks, rows, tile)

        start(1, late_total, late_out)
        arrive(0, sent_ref, fields)

        @pl.loop(0, half // tile)
        def _(step):
            lanes = pl.ds(pl.multiple_of(step * tile, tile), tile)
            beyond = pl.ds(pl.multiple_of(half + step * tile, tile), tile)
            first = fields[:, :, lanes]
            total = product(matrix_ref[...], first)
            early_total[:, :, lanes] = total.reshape(blocks, rows, tile)
            total = product(matrix_ref[...], fields[:, :, beyond]) + product(
                episode_ref[...], first
            )
            early_total[:, :, beyond] = total.reshape(blocks, rows, tile)

        start(2, early_total, early_out)
        arrive(1, late_total, late_out)
        arrive(2, early_total, early_out)
        leave(0, sent_ref, fields)
        leave(1, late_total, late_out)
        leave(2, early_total, early_out)

    shape = jax.ShapeDtypeStruct(sent_early.shape, jnp.float32)
    vmem = pl.BlockSpec(memory_space=pltpu.VMEM)
    anywhere = pl.BlockSpec(memory_space=pl.ANY)
    buffer = pltpu.VMEM(sent_early.shape, jnp.float32)
    return pl.pallas_call(
        kernel,
        in_specs=[vmem, vmem, vmem, anywhere],
        out_specs=[anywhere, anywhere],
        out_shape=[shape, shape],
        scratch_shapes=[
            buffer,
            buffer,
            buffer,
            pltpu.SemaphoreType.DMA((3, blocks)),
            pltpu.SemaphoreType.DMA((3, blocks)),
            pltpu.SemaphoreType.DMA((3,)),
        ],
        compiler_params=pltpu.CompilerParams(
            collective_id=0, has_side_effects=True, vmem_limit_bytes=VMEM_LIMIT
        ),
        cost_estimate=pl.CostEstimate(
            flops=6 * breadth * breadth * wide,
            bytes_accessed=24 * breadth * wide,
            transcendentals=0,
        ),
    )(matrix, episodes, came_late, sent_early)


def local(
    starting_joint_sensitivities,
    former_section_velocity,
    nominal_coefficient_factors,
    unlocking_coefficients_by_grade,
    repression_grade_by_abundance,
    measured_outbreak_frequencies,
    upper_bounds_per_abundance,
):
    start, velocity = starting_joint_sensitivities, former_section_velocity
    comps, genes, rows, cells = start.shape
    blocks = lax.axis_size("slab")
    width = cells // blocks
    breadth = measured_outbreak_frequencies.shape[0]
    rates = nominal_coefficient_factors * jnp.array(nominal_coefficient_basis, dtype=jnp.float32)
    burst, trans, off, mdecay, decay1, make2, decay2 = [rates[place] for place in range(7)]
    bound = jnp.broadcast_to(upper_bounds_per_abundance[:, None], (rows, 128))

    bound_cells = bound * P2

    def exchanged(value):
        return lax.all_to_all(value, "slab", split_axis=0, concat_axis=0, tiled=True)

    first_index = jnp.arange(cells, dtype=jnp.int32) // P2
    lowest = start[:, 0, 0, :] + section_step * velocity[:, 0, 0, :]
    lowest = jnp.where(first_index[None, :] < upper_bounds_per_abundance[0], lowest, 0.0)
    halo = shifted(lowest, "slab", -1)
    sent_late, halo = lax.optimization_barrier(
        (on_state(start, velocity, bound_cells, 1, blocks), halo)
    )
    came_late = exchanged(sent_late)
    sent_early = on_state(start, velocity, bound_cells, 0, blocks)

    first_row = lax.axis_index("slab") * rows
    m_count = (first_row + jnp.arange(rows, dtype=jnp.int32)).astype(jnp.float32)
    c_count = jnp.arange(P2, dtype=jnp.float32)
    kon = kon_rates(unlocking_coefficients_by_grade, repression_grade_by_abundance)
    row_rates = jnp.concatenate(
        [
            jnp.broadcast_to((trans * m_count)[:, None], (rows, 128)),
            jnp.broadcast_to((mdecay * (m_count + 1.0))[:, None], (rows, 128)),
        ],
        axis=1,
    )
    shared = -((trans * m_count)[:, None] + (decay2 * c_count)[None, :])
    diagonals = jnp.stack(
        [shared - (mdecay * m_count)[:, None] - kon[None, :], shared - off], axis=0
    )
    columns = jnp.zeros((8, P2), jnp.float32)
    columns = columns.at[0].set(kon)
    columns = columns.at[1].set((c_count >= 1.0).astype(jnp.float32))
    columns = columns.at[2].set(jnp.where(c_count < P2 - 1.0, decay2 * (c_count + 1.0), 0.0))
    slope = partial_slope(start, velocity, halo, rates, bound, row_rates, diagonals, columns)

    unit = jnp.eye(breadth, dtype=jnp.float32)
    m_all = jnp.arange(breadth, dtype=jnp.float32)
    episodes = burst * (episode_share_stencil(measured_outbreak_frequencies, breadth) - unit)
    removal = mdecay * (
        (m_all + 1.0)[:, None] * jnp.eye(breadth, k=1, dtype=jnp.float32) - m_all[:, None] * unit
    )
    matrix = episodes + removal

    came_late, sent_early, slope = lax.optimization_barrier((came_late, sent_early, slope))
    returned_late, returned_early = exchange_rest(matrix, episodes, came_late, sent_early, rows)
    return add_rows(slope, returned_early, returned_late, bound_cells)


def solution(mesh):
    placed = (
        P("ens", None, "slab", None),
        P("ens", None, "slab", None),
        P("ens"),
        P("ens"),
        P(),
        P(),
        P("slab"),
    )
    return jax.shard_map(
        local, mesh=mesh, in_specs=placed, out_specs=P("ens", None, "slab", None), check_vma=False
    )
```
